32 devices in a mesh: groups: 2 (over x), chan: 16 (over z, y, core).
Axes of the slice: x: 2, y: 2, z: 4, core: 2. Of those that a mesh axis runs over, the one named last changes fastest.
Arguments:
- voltages: bfloat16 [4, 256, 16, 8192], P(None, 'chan', 'groups'), parts along dimension 2, may hold values from -3 to 3
- jones_terms: bfloat16 [16, 256, 8192], P('groups', 'chan'), parts along dimension 0, may hold values from -3 to 3
- rfi_flags: int32 [16, 8192], P('groups', 'chan'), parts along dimension 0, may hold values from 0 to 1, as said below
- delay_ticks: int32 [256, 256], replicated, may hold values from 0 to 8191
Outputs:
- beam_power: float32 [256, 16384], P('chan', 'groups'), parts along dimension 1
The draws below stay inside these ranges and needn't reach their ends.
There are 2 independent parts, one for each index of `groups`. The reference program is written for one: setup_inputs(seed, part) draws one part's arguments, and reference() takes and returns one part's arrays. A program takes and returns all parts, laid end to end along the dimension named above; an argument that names none is the same for every part. Nothing has to cross between parts.
Inputs may be any that keep to these rules, and one draw needn't show every extreme that they name: `rfi_flags`: in every draw some channels are flagged at all 8 samples.
All inputs are finite; a program needn't handle non-finite values.
Results may differ from the reference program's by a relative error of at most 0.0017.
Values may be sent and summed in bfloat16 or wider, within the bound.
A program may use at most 256 MiB of HBM per device.

```python
import math
import jax
import jax.numpy as jnp
from jax import lax

STATIONS = 256
CHANNELS = 8192
BEAMS = 256
TSAMP = 8


def draw_rfi_flags(key, part):
    key = jax.random.fold_in(key, 11)
    dead_key, sample_key, pick_key, band_key = jax.random.split(key, 4)
    dead = jax.random.randint(dead_key, (CHANNELS,), 0, 8) == 0
    chosen = jax.random.randint(pick_key, (), 0, CHANNELS)
    dead = dead | (jnp.arange(CHANNELS) == chosen)
    band_rate = jax.random.randint(band_key, (CHANNELS,), 1, 5)
    sample = jax.random.randint(sample_key, (TSAMP, CHANNELS), 0, 8) < band_rate[None, :]
    return jnp.where(dead[None, :] | sample, 1, 0).astype(jnp.int32)


def with_ends(drawn, rng, least, top_value):
    dims = drawn.shape
    spot = [jax.random.randint(jax.random.fold_in(rng, axis), (), 0, dims[axis]) for axis in range(len(dims))]
    drawn = drawn.at[tuple(spot)].set(least)
    longest = dims.index(max(dims))
    spot[longest] = (spot[longest] + 1) % dims[longest]
    return drawn.at[tuple(spot)].set(top_value)


def level_of(stream_key, extent, cuts, least, largest):
    gain, own = 1.0, jax.random.fold_in(stream_key, 6)
    for position, shards_of in cuts:
        draws = jnp.exp(jax.random.uniform(jax.random.fold_in(own, position), (shards_of,), jnp.float32, least / len(cuts), largest / len(cuts)))
        gain = gain * jnp.repeat(draws, extent[position] // shards_of).reshape([-1 if axis == position else 1 for axis in range(len(extent))])
    return gain


def noise(rng, dims, width, limit, shards=(), held_as=jnp.bfloat16):
    drawn = jax.random.normal(rng, dims, jnp.float32) * width
    if len(shards) > 0:
        drawn = level_of(rng, dims, shards, -0.22, 0.18) * drawn
    return jnp.clip(drawn, min=-limit, max=limit).astype(held_as)


def setup_inputs(seed: int = 0, part: int = 0) -> dict:
    key_list = jax.random.split(jax.random.key(seed), 5)
    part_splits = jax.random.split(jax.random.fold_in(key_list[4], part), 5)
    voltages = noise(part_splits[0], (4, STATIONS, TSAMP, CHANNELS), 0.5, 3.0, ((1, 16),))
    jones_terms = noise(part_splits[1], (8, STATIONS, CHANNELS), 0.5, 3.0, ((1, 16),))
    rfi_flags = draw_rfi_flags(jax.random.fold_in(jax.random.fold_in(key_list[4], part), 71), part)
    delay_ticks = with_ends(jax.random.randint(key_list[3], (BEAMS, STATIONS), 0, CHANNELS), jax.random.fold_in(key_list[3], 1), 0, CHANNELS - 1).astype(jnp.int32)
    return {"voltages": voltages, "jones_terms": jones_terms, "rfi_flags": rfi_flags, "delay_ticks": delay_ticks}


def apply_jones(volt_block, jones_block):
    volt_parts = [volt_block[k].astype(jnp.float32) for k in range(4)]
    jones_parts = [jones_block[k].astype(jnp.float32) for k in range(8)]
    outputs = []
    for target in range(2):
        real_sum = jnp.zeros_like(volt_parts[0])
        imag_sum = jnp.zeros_like(volt_parts[0])
        for source in range(2):
            jones_re = jones_parts[4 * target + 2 * source]
            jones_im = jones_parts[4 * target + 2 * source + 1]
            volt_re = volt_parts[2 * source]
            volt_im = volt_parts[2 * source + 1]
            real_sum = real_sum + jones_re * volt_re - jones_im * volt_im
            imag_sum = imag_sum + jones_re * volt_im + jones_im * volt_re
        outputs.append(real_sum)
        outputs.append(imag_sum)
    return jnp.stack(outputs).astype(jnp.bfloat16)

def reference(voltages, jones_terms, rfi_flags, delay_ticks):
    block_size = min(64, CHANNELS)
    block_count = CHANNELS // block_size
    weight_scale = 1.0 / math.sqrt(STATIONS)

    def one_block(first_chan):
        volt_block = lax.dynamic_slice_in_dim(voltages, first_chan, block_size, 3)
        jones_block = lax.dynamic_slice_in_dim(jones_terms, first_chan, block_size, 2)
        flag_block = lax.dynamic_slice_in_dim(rfi_flags, first_chan, block_size, 1)
        corrected = apply_jones(volt_block, jones_block[:, :, None, :])
        chan_ids = (first_chan + jnp.arange(block_size)).astype(jnp.int32)
        turns = delay_ticks[None, :, :] * chan_ids[:, None, None] % CHANNELS
        phase_angle = turns.astype(jnp.float32) * (2.0 * math.pi / CHANNELS)
        weights = jnp.stack([jnp.cos(phase_angle) * weight_scale, -jnp.sin(phase_angle) * weight_scale]).astype(jnp.bfloat16)
        products = jnp.einsum('wcbs,kstc->wkbtc', weights.astype(jnp.float32), corrected.astype(jnp.float32), precision=lax.Precision.HIGHEST)
        x_re = products[0, 0] - products[1, 1]
        x_im = products[0, 1] + products[1, 0]
        y_re = products[0, 2] - products[1, 3]
        y_im = products[0, 3] + products[1, 2]
        sample_power = x_re * x_re + x_im * x_im + y_re * y_re + y_im * y_im
        kept_mask = (1 - flag_block).astype(jnp.float32)
        summed = lax.optimization_barrier(jnp.sum(sample_power * kept_mask[None, :, :], axis=1))
        kept_count = lax.optimization_barrier(jnp.sum(kept_mask, axis=0))
        return summed / jnp.maximum(kept_count, 1.0)[None, :]
    starts = (jnp.arange(block_count) * block_size).astype(jnp.int32)
    blocks = lax.map(one_block, starts)
    return jnp.moveaxis(blocks, 0, 1).reshape(BEAMS, CHANNELS)
```

```python
import functools
import math

import jax
import jax.numpy as jnp
from jax import lax
from jax.experimental import pallas as pl
from jax.experimental.pallas import tpu as pltpu
from jax.sharding import PartitionSpec as P

LANES = 128
PAIRS = 8


def kernel(dims, volt_hbm, jones_hbm, flags, ticks, out, volt, jones, jones_f, send, recv, wide,
           turned, base, table, power, out_send, out_recv, volt_sem, jones_sem,
           send_sem, recv_sem, osend_sem, orecv_sem):
    n, s_loc, tsamp, chunks, beams, stations, channels = dims
    rows = 4 * tsamp
    width = chunks * LANES
    b_loc = beams // n
    me = lax.axis_index("chan")

    def partner(i):
        step = (i + 1) // 2
        off = n // 2 + jnp.where(i % 2 == 1, -step, step)
        return lax.rem(me + off + n, n)

    def load(j):
        cols = pl.ds(pl.multiple_of(j * width, LANES), width)
        return (
            pltpu.make_async_copy(volt_hbm.at[:, cols], volt.at[:, cols], volt_sem.at[j]),
            pltpu.make_async_copy(jones_hbm.at[:, cols], jones.at[:, cols], jones_sem.at[j]),
        )

    @pl.loop(0, n)
    def _(i):
        for copy in load(partner(i)):
            copy.start()

    barrier = pltpu.get_barrier_semaphore()

    @pl.loop(0, n - 1)
    def _(i):
        pl.semaphore_signal(barrier, inc=1, device_id={"chan": partner(i)},
                            device_id_type=pl.DeviceIdType.MESH)

    pl.semaphore_wait(barrier, n - 1)

    def volt_copy(q, j, origin):
        return pltpu.make_async_remote_copy(
            src_ref=send.at[q, j], dst_ref=recv.at[q, origin],
            send_sem=send_sem.at[q, j], recv_sem=recv_sem.at[q, origin],
            device_id={"chan": j}, device_id_type=pl.DeviceIdType.MESH)

    def power_copy(q, j, origin):
        return pltpu.make_async_remote_copy(
            src_ref=out_send.at[q, j], dst_ref=out_recv.at[q, origin],
            send_sem=osend_sem.at[q, j], recv_sem=orecv_sem.at[q, origin],
            device_id={"chan": j}, device_id_type=pl.DeviceIdType.MESH)

    def correct(q, j, put):
        cols = pl.ds(pl.multiple_of(j * width + q * LANES, LANES), LANES)
        jones_f[...] = jones[:, cols].astype(jnp.float32)
        for s in range(0, s_loc, 2):
            v = [volt[pl.ds(k * s_loc * tsamp + s * tsamp, 2 * tsamp), cols].astype(jnp.float32)
                 for k in range(4)]
            for e in range(2):
                ve = [a[e * tsamp:(e + 1) * tsamp] for a in v]
                m = [jnp.broadcast_to(jones_f[pl.ds(i * s_loc + s + e, 1), :], (tsamp, LANES))
                     for i in range(8)]
                done = []
                for o in range(2):
                    r0, i0, r1, i1 = m[4 * o:4 * o + 4]
                    done.append(r0 * ve[0] - i0 * ve[1] + r1 * ve[2] - i1 * ve[3])
                    done.append(r0 * ve[1] + i0 * ve[0] + r1 * ve[3] + i1 * ve[2])
                put(s + e, jnp.concatenate(done, axis=0).astype(jnp.bfloat16))

    @pl.loop(0, chunks)
    def _(q):
        @pl.loop(0, n)
        def _(i):
            j = partner(i)

            @pl.when(q == 0)
            def _():
                for copy in load(j):
                    copy.wait()

            def put(s, value):
                send[q, j, s] = value

            correct(q, j, put)

            @pl.when(i < n - 1)
            def _():
                volt_copy(q, j, me).start()

    scale = 1.0 / math.sqrt(stations)

    def turn(part, twice):
        t = lax.rem(part * twice, 2 * channels)
        t = jnp.where(t >= channels, t - 2 * channels, t)
        angle = t.astype(jnp.float32) * (math.pi / channels)
        return jnp.cos(angle), -jnp.sin(angle)

    def mul(a, b):
        return a[0] * b[0] - a[1] * b[1], a[0] * b[1] + a[1] * b[0]

    @pl.loop(0, stations // 16)
    def _(i):
        at = pl.ds(pl.multiple_of(i * 16, 16), 16)
        part = ticks[at, :]
        first = turn(part, me * (2 * width) + 2 * PAIRS - 1)
        base[0, at, :] = first[0] * scale
        base[1, at, :] = first[1] * scale
        jump = turn(part, 4 * PAIRS)
        table[PAIRS, 0, at, :] = jump[0]
        table[PAIRS, 1, at, :] = jump[1]
        half = turn(part, 1)
        one = turn(part, 2)
        for k in range(PAIRS):
            table[k, 0, at, :] = half[0]
            table[k, 1, at, :] = half[1]
            half = mul(half, one)

    @pl.loop(0, chunks)
    def _(q):
        @pl.loop(0, n - 1)
        def _(i):
            volt_copy(q, partner(i), partner(i)).wait_recv()

        kept = (1 - flags[:, pl.ds(pl.multiple_of(q * LANES, LANES), LANES)]).astype(jnp.float32)
        mask = jnp.concatenate([kept] * 4, axis=0)

        def widen(j, ref):
            @pl.loop(0, s_loc // 2)
            def _(s):
                for e in range(2):
                    at = pl.multiple_of((j * s_loc + 2 * s + e) * rows, rows)
                    wide[pl.ds(at, rows), :] = ref[2 * s + e].astype(jnp.float32) * mask

        @pl.loop(0, n - 1)
        def _(i):
            j = partner(i)
            widen(j, recv.at[q, j])

        widen(me, send.at[q, me])

        halves = stations // LANES

        @pl.loop(0, rows)
        def _(r):
            for h in range(halves):
                got = wide[pl.ds(h * LANES * rows + r, LANES, stride=rows), :]
                turned[h, pl.ds(r, LANES, stride=rows), :] = got.T

        @pl.loop(0, LANES // (2 * PAIRS))
        def _(g):
            @pl.loop(0, PAIRS)
            def _(k):
                a, b = base[0], base[1]
                c, d = table[k, 0], table[k, 1]
                ac, bd, ad, bc = a * c, b * d, a * d, b * c
                for up in (True, False):
                    if up:
                        wr, wi, chan = ac - bd, ad + bc, g * (2 * PAIRS) + PAIRS + k
                    else:
                        wr, wi, chan = ac + bd, bc - ad, g * (2 * PAIRS) + PAIRS - 1 - k
                    at = pl.ds(pl.multiple_of(chan * rows, rows), rows)
                    x = jnp.concatenate([turned[h, at, :] for h in range(halves)], axis=1)
                    y = jnp.concatenate([-x[tsamp:2 * tsamp], x[:tsamp],
                                         -x[3 * tsamp:], x[2 * tsamp:3 * tsamp]], axis=0)
                    z = jnp.dot(x.astype(jnp.bfloat16), wr.astype(jnp.bfloat16),
                                preferred_element_type=jnp.float32)
                    z += jnp.dot(y.astype(jnp.bfloat16), wi.astype(jnp.bfloat16),
                                 preferred_element_type=jnp.float32)
                    power[pl.ds(chan, 1), :] = jnp.sum(z * z, axis=0, keepdims=True)

            @pl.loop(0, stations // 16)
            def _(i):
                at = pl.ds(pl.multiple_of(i * 16, 16), 16)
                moved = mul((base[0, at, :], base[1, at, :]),
                            (table[PAIRS, 0, at, :], table[PAIRS, 1, at, :]))
                base[0, at, :] = moved[0]
                base[1, at, :] = moved[1]

        count = jnp.maximum(jnp.sum(kept, axis=0, keepdims=True), 1.0)
        result = power[...].T / count
        for j in range(n):
            out_send[q, j, 0:b_loc, :] = result[j * b_loc:(j + 1) * b_loc]

        @pl.loop(0, n - 1)
        def _(i):
            power_copy(q, partner(i), me).start()

    @pl.loop(0, chunks)
    def _(q):
        out[:, pl.ds(pl.multiple_of(me * width + q * LANES, LANES), LANES)] = out_send[q, me, 0:b_loc, :]

        @pl.loop(0, n - 1)
        def _(i):
            j = partner(i)
            power_copy(q, j, j).wait_recv()
            out[:, pl.ds(pl.multiple_of(j * width + q * LANES, LANES), LANES)] = out_recv[q, j, 0:b_loc, :]
            power_copy(q, j, me).wait_send()
            volt_copy(q, j, me).wait_send()


def local(n, voltages, jones_terms, rfi_flags, delay_ticks):
    _, s_loc, tsamp, channels = voltages.shape
    beams, stations = delay_ticks.shape
    chunks = channels // n // LANES
    b_loc = beams // n
    b_pad = -(-b_loc // 8) * 8
    rows = 4 * tsamp
    dims = (n, s_loc, tsamp, chunks, beams, stations, channels)
    f32, bf16 = jnp.float32, jnp.bfloat16
    anywhere = pl.BlockSpec(memory_space=pl.ANY)
    vmem = pl.BlockSpec(memory_space=pltpu.VMEM)
    dma = pltpu.SemaphoreType.DMA
    return pl.pallas_call(
        functools.partial(kernel, dims),
        out_shape=jax.ShapeDtypeStruct((b_loc, channels), f32),
        in_specs=[anywhere, anywhere, vmem, vmem],
        out_specs=vmem,
        scratch_shapes=[
            pltpu.VMEM((4 * s_loc * tsamp, channels), bf16),
            pltpu.VMEM((8 * s_loc, channels), bf16),
            pltpu.VMEM((8 * s_loc, LANES), f32),
            pltpu.VMEM((chunks, n, s_loc, rows, LANES), bf16),
            pltpu.VMEM((chunks, n, s_loc, rows, LANES), bf16),
            pltpu.VMEM((stations * rows, LANES), f32),
            pltpu.VMEM((stations // LANES, LANES * rows, LANES), f32),
            pltpu.VMEM((2, stations, beams), f32),
            pltpu.VMEM((PAIRS + 1, 2, stations, beams), f32),
            pltpu.VMEM((LANES, beams), f32),
            pltpu.VMEM((chunks, n, b_pad, LANES), f32),
            pltpu.VMEM((chunks, n, b_pad, LANES), f32),
            dma((n,)), dma((n,)),
            dma((chunks, n)), dma((chunks, n)), dma((chunks, n)), dma((chunks, n)),
        ],
        compiler_params=pltpu.CompilerParams(
            collective_id=0, has_side_effects=True, vmem_limit_bytes=56 * 1024 * 1024),
    )(
        voltages.reshape(4 * s_loc * tsamp, channels),
        jones_terms.reshape(8 * s_loc, channels),
        rfi_flags,
        delay_ticks.T,
    )


def solution(mesh):
    return jax.shard_map(
        functools.partial(local, mesh.shape["chan"]),
        mesh=mesh,
        in_specs=(
            P(None, "chan", "groups", None),
            P("groups", "chan", None),
            P("groups", "chan"),
            P(),
        ),
        out_specs=P("chan", "groups"),
        check_vma=False,
    )
```

```python
import functools
import math

import jax
import jax.numpy as jnp
from jax import lax
from jax.experimental import pallas as pl
from jax.experimental.pallas import tpu as pltpu
from jax.sharding import PartitionSpec as P

LANES = 128
PAIRS = 8
PITCH = 40
UNROLL = 8


def kernel(dims, volt_hbm, jones_hbm, flags, ticks, out, volt, jones, jones_f, send, recv, wide,
           turned, ticks_t, partial, base, table, power, out_send, out_recv, volt_sem, jones_sem,
           send_sem, recv_sem, osend_sem, orecv_sem):
    n, s_loc, tsamp, chunks, beams, stations, channels = dims
    rows = 4 * tsamp
    width = chunks * LANES
    b_loc = beams // n
    me = lax.axis_index("chan")
    half = n // 2
    side, place = me // half, lax.rem(me, half)

    def partner(i):
        step = (i + 1) // 2
        return jnp.where(i % 2 == 0, (1 - side) * half + lax.rem(place + step, half),
                         side * half + lax.rem(place + step, half))

    def load(j):
        cols = pl.ds(pl.multiple_of(j * width, LANES), width)
        return (
            pltpu.make_async_copy(volt_hbm.at[:, cols], volt.at[:, cols], volt_sem.at[j]),
            pltpu.make_async_copy(jones_hbm.at[:, cols], jones.at[:, cols], jones_sem.at[j]),
        )

    barrier = pltpu.get_barrier_semaphore()

    @pl.loop(0, n - 1)
    def _(i):
        pl.semaphore_signal(barrier, inc=1, device_id={"chan": partner(i)},
                            device_id_type=pl.DeviceIdType.MESH)

    @pl.loop(0, n)
    def _(i):
        for copy in load(partner(i)):
            copy.start()

    pl.semaphore_wait(barrier, n - 1)

    def volt_copy(q, j, origin):
        return pltpu.make_async_remote_copy(
            src_ref=send.at[q, j], dst_ref=recv.at[q, origin],
            send_sem=send_sem.at[q, j], recv_sem=recv_sem.at[q, origin],
            device_id={"chan": j}, device_id_type=pl.DeviceIdType.MESH)

    def power_copy(q, j, origin):
        return pltpu.make_async_remote_copy(
            src_ref=out_send.at[q, j], dst_ref=out_recv.at[q, origin],
            send_sem=osend_sem.at[q, j], recv_sem=orecv_sem.at[q, origin],
            device_id={"chan": j}, device_id_type=pl.DeviceIdType.MESH)

    def correct(q, j, put):
        cols = pl.ds(pl.multiple_of(j * width + q * LANES, LANES), LANES)
        jones_f[...] = jones[:, cols].astype(jnp.float32)
        for s in range(0, s_loc, 2):
            v = [volt[pl.ds(k * s_loc * tsamp + s * tsamp, 2 * tsamp), cols].astype(jnp.float32)
                 for k in range(4)]
            for e in range(2):
                ve = [a[e * tsamp:(e + 1) * tsamp] for a in v]
                m = [jnp.broadcast_to(jones_f[pl.ds(i * s_loc + s + e, 1), :], (tsamp, LANES))
                     for i in range(8)]
                done = []
                for o in range(2):
                    r0, i0, r1, i1 = m[4 * o:4 * o + 4]
                    done.append(r0 * ve[0] - i0 * ve[1] + r1 * ve[2] - i1 * ve[3])
                    done.append(r0 * ve[1] + i0 * ve[0] + r1 * ve[3] + i1 * ve[2])
                put(s + e, jnp.concatenate(done, axis=0).astype(jnp.bfloat16))

    @pl.loop(0, chunks)
    def _(q):
        @pl.loop(0, n)
        def _(i):
            j = partner(i)

            @pl.when(q == 0)
            def _():
                for copy in load(j):
                    copy.wait()

            def put(s, value):
                send[q, j, s] = value

            correct(q, j, put)

            @pl.when(i < n - 1)
            def _():
                volt_copy(q, j, me).start()

    scale = 1.0 / math.sqrt(stations)

    def turn(part, twice):
        t = lax.rem(part * twice, 2 * channels)
        t = jnp.where(t >= channels, t - 2 * channels, t)
        angle = t.astype(jnp.float32) * (math.pi / channels)
        return jnp.cos(angle), -jnp.sin(angle)

    def mul(a, b):
        return a[0] * b[0] - a[1] * b[1], a[0] * b[1] + a[1] * b[0]

    ticks_t[...] = ticks[...].T

    @pl.loop(0, stations // 16)
    def _(i):
        at = pl.ds(pl.multiple_of(i * 16, 16), 16)
        part = ticks_t[at, :]
        first = turn(part, me * (2 * width) + 2 * PAIRS - 1)
        base[0, at, :] = first[0] * scale
        base[1, at, :] = first[1] * scale
        jump = turn(part, 4 * PAIRS)
        table[PAIRS, 0, at, :] = jump[0]
        table[PAIRS, 1, at, :] = jump[1]
        half = turn(part, 1)
        one = turn(part, 2)
        for k in range(PAIRS):
            table[k, 0, at, :] = half[0]
            table[k, 1, at, :] = half[1]
            half = mul(half, one)

    def gather(q, h, own):
        kept = (1 - flags[:, pl.ds(pl.multiple_of(q * LANES, LANES), LANES)]).astype(jnp.float32)
        mask = jnp.concatenate([kept] * 4, axis=0)

        def widen(j, ref):
            @pl.loop(0, s_loc, unroll=min(s_loc, 8))
            def _(s):
                at = pl.multiple_of((lax.rem(j, half) * s_loc + s) * PITCH, 8)
                wide[pl.ds(at, rows), :] = ref[s].astype(jnp.float32) * mask

        @pl.loop(0, half - 1 if own else half)
        def _(i):
            j = h * half + lax.rem(place + (i + 1 if own else i), half)
            volt_copy(q, j, j).wait_recv()
            widen(j, recv.at[q, j])

        if own:
            widen(me, send.at[q, me])

        @pl.loop(0, rows, unroll=4)
        def _(r):
            got = wide[pl.ds(r, LANES, stride=PITCH), :]
            turned[pl.ds(r, LANES, stride=PITCH), :] = got.T

    def combine(h, own):
        members = pl.ds(pl.multiple_of(h * LANES, LANES), LANES)

        @pl.loop(0, LANES // (2 * PAIRS))
        def _(g):
            @pl.loop(0, PAIRS, unroll=UNROLL)
            def _(k):
                a, b = base[0, members, :], base[1, members, :]
                c, d = table[k, 0, members, :], table[k, 1, members, :]
                ac, bd, ad, bc = a * c, b * d, a * d, b * c
                for up in (True, False):
                    if up:
                        wr, wi, chan = ac - bd, ad + bc, g * (2 * PAIRS) + PAIRS + k
                    else:
                        wr, wi, chan = ac + bd, bc - ad, g * (2 * PAIRS) + PAIRS - 1 - k
                    x = turned[pl.ds(pl.multiple_of(chan * PITCH, 8), rows), :]
                    y = jnp.concatenate([-x[tsamp:2 * tsamp], x[:tsamp],
                                         -x[3 * tsamp:], x[2 * tsamp:3 * tsamp]], axis=0)
                    w = jnp.concatenate([wr.astype(jnp.bfloat16), wi.astype(jnp.bfloat16)], axis=0)
                    z = jnp.dot(jnp.concatenate([x, y], axis=1).astype(jnp.bfloat16), w,
                                preferred_element_type=jnp.float32)
                    at = pl.ds(pl.multiple_of(chan * rows, rows), rows)
                    if own:
                        partial[at, :] = z
                    else:
                        z += partial[at, :]
                        power[pl.ds(chan, 1), :] = jnp.sum(z * z, axis=0, keepdims=True)

            @pl.loop(0, LANES // 16)
            def _(i):
                at = pl.ds(pl.multiple_of(h * LANES + i * 16, 16), 16)
                moved = mul((base[0, at, :], base[1, at, :]),
                            (table[PAIRS, 0, at, :], table[PAIRS, 1, at, :]))
                base[0, at, :] = moved[0]
                base[1, at, :] = moved[1]

    @pl.loop(0, chunks)
    def _(q):
        gather(q, side, True)
        combine(side, True)
        gather(q, 1 - side, False)
        combine(1 - side, False)
        kept = (1 - flags[:, pl.ds(pl.multiple_of(q * LANES, LANES), LANES)]).astype(jnp.float32)
        count = jnp.maximum(jnp.sum(kept, axis=0, keepdims=True), 1.0)
        result = power[...].T / count
        for j in range(n):
            out_send[q, j, 0:b_loc, :] = result[j * b_loc:(j + 1) * b_loc]

        @pl.loop(0, n - 1)
        def _(i):
            power_copy(q, partner(i), me).start()

    @pl.loop(0, chunks)
    def _(q):
        out[:, pl.ds(pl.multiple_of(me * width + q * LANES, LANES), LANES)] = out_send[q, me, 0:b_loc, :]

        @pl.loop(0, n - 1)
        def _(i):
            j = partner(i)
            power_copy(q, j, j).wait_recv()
            out[:, pl.ds(pl.multiple_of(j * width + q * LANES, LANES), LANES)] = out_recv[q, j, 0:b_loc, :]
            power_copy(q, j, me).wait_send()
            volt_copy(q, j, me).wait_send()


def local(n, voltages, jones_terms, rfi_flags, delay_ticks):
    _, s_loc, tsamp, channels = voltages.shape
    beams, stations = delay_ticks.shape
    chunks = channels // n // LANES
    b_loc = beams // n
    b_pad = -(-b_loc // 8) * 8
    rows = 4 * tsamp
    dims = (n, s_loc, tsamp, chunks, beams, stations, channels)
    f32, bf16 = jnp.float32, jnp.bfloat16
    anywhere = pl.BlockSpec(memory_space=pl.ANY)
    vmem = pl.BlockSpec(memory_space=pltpu.VMEM)
    dma = pltpu.SemaphoreType.DMA
    return pl.pallas_call(
        functools.partial(kernel, dims),
        out_shape=jax.ShapeDtypeStruct((b_loc, channels), f32),
        in_specs=[anywhere, anywhere, vmem, vmem],
        out_specs=vmem,
        scratch_shapes=[
            pltpu.VMEM((4 * s_loc * tsamp, channels), bf16),
            pltpu.VMEM((8 * s_loc, channels), bf16),
            pltpu.VMEM((8 * s_loc, LANES), f32),
            pltpu.VMEM((chunks, n, s_loc, rows, LANES), bf16),
            pltpu.VMEM((chunks, n, s_loc, rows, LANES), bf16),
            pltpu.VMEM((LANES * PITCH, LANES), f32),
            pltpu.VMEM((LANES * PITCH, LANES), f32),
            pltpu.VMEM((stations, beams), jnp.int32),
            pltpu.VMEM((LANES * rows, beams), f32),
            pltpu.VMEM((2, stations, beams), f32),
            pltpu.VMEM((PAIRS + 1, 2, stations, beams), f32),
            pltpu.VMEM((LANES, beams), f32),
            pltpu.VMEM((chunks, n, b_pad, LANES), f32),
            pltpu.VMEM((chunks, n, b_pad, LANES), f32),
            dma((n,)), dma((n,)),
            dma((chunks, n)), dma((chunks, n)), dma((chunks, n)), dma((chunks, n)),
        ],
        compiler_params=pltpu.CompilerParams(
            collective_id=0, has_side_effects=True, vmem_limit_bytes=56 * 1024 * 1024),
    )(
        voltages.reshape(4 * s_loc * tsamp, channels),
        jones_terms.reshape(8 * s_loc, channels),
        rfi_flags,
        delay_ticks,
    )


def solution(mesh):
    return jax.shard_map(
        functools.partial(local, mesh.shape["chan"]),
        mesh=mesh,
        in_specs=(
            P(None, "chan", "groups", None),
            P("groups", "chan", None),
            P("groups", "chan"),
            P(),
        ),
        out_specs=P("chan", "groups"),
        check_vma=False,
    )
```

```python
import functools
import math

import jax
import jax.numpy as jnp
from jax import lax
from jax.experimental import pallas as pl
from jax.experimental.pallas import tpu as pltpu
from jax.sharding import PartitionSpec as P

LANES = 128
PAIRS = 8
PITCH = 40
UNROLL = 8


def kernel(dims, volt_hbm, jones_hbm, flags, ticks, out, volt, jones, jones_f, send, recv, wide,
           turned, ticks_t, partial, base, table, power, out_send, out_recv, volt_sem, jones_sem,
           send_sem, recv_sem, osend_sem, orecv_sem):
    n, s_loc, tsamp, chunks, beams, stations, channels = dims
    rows = 4 * tsamp
    width = chunks * LANES
    b_loc = beams // n
    me = lax.axis_index("chan")
    half = n // 2
    side, place = me // half, lax.rem(me, half)

    def partner(i):
        step = (i + 1) // 2
        return jnp.where(i % 2 == 0, (1 - side) * half + lax.rem(place + step, half),
                         side * half + lax.rem(place + step, half))

    def load(j):
        cols = pl.ds(pl.multiple_of(j * width, LANES), width)
        return (
            pltpu.make_async_copy(volt_hbm.at[:, cols], volt.at[:, cols], volt_sem.at[j]),
            pltpu.make_async_copy(jones_hbm.at[:, cols], jones.at[:, cols], jones_sem.at[j]),
        )

    barrier = pltpu.get_barrier_semaphore()

    @pl.loop(0, n - 1)
    def _(i):
        pl.semaphore_signal(barrier, inc=1, device_id={"chan": partner(i)},
                            device_id_type=pl.DeviceIdType.MESH)

    @pl.loop(0, n)
    def _(i):
        for copy in load(partner(i)):
            copy.start()

    pl.semaphore_wait(barrier, n - 1)

    def volt_copy(q, j, origin):
        return pltpu.make_async_remote_copy(
            src_ref=send.at[q, j], dst_ref=recv.at[q, origin],
            send_sem=send_sem.at[q, j], recv_sem=recv_sem.at[q, origin],
            device_id={"chan": j}, device_id_type=pl.DeviceIdType.MESH)

    def power_copy(q, j, origin):
        return pltpu.make_async_remote_copy(
            src_ref=out_send.at[q, j], dst_ref=out_recv.at[q, origin],
            send_sem=osend_sem.at[q, j], recv_sem=orecv_sem.at[q, origin],
            device_id={"chan": j}, device_id_type=pl.DeviceIdType.MESH)

    def correct(q, j, put):
        cols = pl.ds(pl.multiple_of(j * width + q * LANES, LANES), LANES)
        jones_f[...] = jones[:, cols].astype(jnp.float32)
        for s in range(0, s_loc, 2):
            v = [volt[pl.ds(k * s_loc * tsamp + s * tsamp, 2 * tsamp), cols].astype(jnp.float32)
                 for k in range(4)]
            for e in range(2):
                ve = [a[e * tsamp:(e + 1) * tsamp] for a in v]
                m = [jnp.broadcast_to(jones_f[pl.ds(i * s_loc + s + e, 1), :], (tsamp, LANES))
                     for i in range(8)]
                done = []
                for o in range(2):
                    r0, i0, r1, i1 = m[4 * o:4 * o + 4]
                    done.append(r0 * ve[0] - i0 * ve[1] + r1 * ve[2] - i1 * ve[3])
                    done.append(r0 * ve[1] + i0 * ve[0] + r1 * ve[3] + i1 * ve[2])
                put(s + e, jnp.concatenate(done, axis=0).astype(jnp.bfloat16))

    @pl.loop(0, chunks)
    def _(q):
        @pl.loop(0, n)
        def _(i):
            j = partner(i)

            @pl.when(q == 0)
            def _():
                for copy in load(j):
                    copy.wait()

            def put(s, value):
                send[q, j, s] = value

            correct(q, j, put)

            @pl.when(i < n - 1)
            def _():
                volt_copy(q, j, me).start()

    scale = 1.0 / math.sqrt(stations)

    def turn(part, twice):
        t = lax.rem(part * twice, 2 * channels)
        t = jnp.where(t >= channels, t - 2 * channels, t)
        angle = t.astype(jnp.float32) * (math.pi / channels)
        return jnp.cos(angle), -jnp.sin(angle)

    def mul(a, b):
        return a[0] * b[0] - a[1] * b[1], a[0] * b[1] + a[1] * b[0]

    ticks_t[...] = ticks[...].T

    @pl.loop(0, stations // 16)
    def _(i):
        at = pl.ds(pl.multiple_of(i * 16, 16), 16)
        part = ticks_t[at, :]
        first = turn(part, me * (2 * width) + 2 * PAIRS - 1)
        base[0, at, :] = first[0] * scale
        base[1, at, :] = first[1] * scale
        jump = turn(part, 4 * PAIRS)
        table[PAIRS, 0, at, :] = jump[0]
        table[PAIRS, 1, at, :] = jump[1]
        half = turn(part, 1)
        one = turn(part, 2)
        for k in range(PAIRS):
            table[k, 0, at, :] = half[0]
            table[k, 1, at, :] = half[1]
            half = mul(half, one)

    def gather(q, h, own):
        kept = (1 - flags[:, pl.ds(pl.multiple_of(q * LANES, LANES), LANES)]).astype(jnp.float32)
        mask = jnp.concatenate([kept] * 4, axis=0)

        def widen(j, ref):
            @pl.loop(0, s_loc, unroll=min(s_loc, 8))
            def _(s):
                at = pl.multiple_of((lax.rem(j, half) * s_loc + s) * PITCH, 8)
                wide[pl.ds(at, rows), :] = ref[s].astype(jnp.float32) * mask

        @pl.loop(0, half - 1 if own else half)
        def _(i):
            j = h * half + lax.rem(place + (i + 1 if own else i), half)
            volt_copy(q, j, j).wait_recv()
            widen(j, recv.at[q, j])

        if own:
            widen(me, send.at[q, me])

        @pl.loop(0, rows, unroll=4)
        def _(r):
            got = wide[pl.ds(r, LANES, stride=PITCH), :]
            turned[pl.ds(r, LANES, stride=PITCH), :] = got.T

    def combine(h, own):
        members = pl.ds(pl.multiple_of(h * LANES, LANES), LANES)

        @pl.loop(0, LANES // (2 * PAIRS))
        def _(g):
            @pl.loop(0, PAIRS, unroll=UNROLL)
            def _(k):
                a, b = base[0, members, :], base[1, members, :]
                c, d = table[k, 0, members, :], table[k, 1, members, :]
                ac, bd, ad, bc = a * c, b * d, a * d, b * c
                for up in (True, False):
                    if up:
                        wr, wi, chan = ac - bd, ad + bc, g * (2 * PAIRS) + PAIRS + k
                    else:
                        wr, wi, chan = ac + bd, bc - ad, g * (2 * PAIRS) + PAIRS - 1 - k
                    x = turned[pl.ds(pl.multiple_of(chan * PITCH, 8), rows), :]
                    y = jnp.concatenate([-x[tsamp:2 * tsamp], x[:tsamp],
                                         -x[3 * tsamp:], x[2 * tsamp:3 * tsamp]], axis=0)
                    w = jnp.concatenate([wr.astype(jnp.bfloat16), wi.astype(jnp.bfloat16)], axis=0)
                    z = jnp.dot(jnp.concatenate([x, y], axis=1).astype(jnp.bfloat16), w,
                                preferred_element_type=jnp.float32)
                    at = pl.ds(pl.multiple_of(chan * rows, rows), rows)
                    if own:
                        partial[at, :] = z
                    else:
                        z += partial[at, :]
                        power[pl.ds(chan, 1), :] = jnp.sum(z * z, axis=0, keepdims=True)

            @pl.loop(0, LANES // 16)
            def _(i):
                at = pl.ds(pl.multiple_of(h * LANES + i * 16, 16), 16)
                moved = mul((base[0, at, :], base[1, at, :]),
                            (table[PAIRS, 0, at, :], table[PAIRS, 1, at, :]))
                base[0, at, :] = moved[0]
                base[1, at, :] = moved[1]

    @pl.loop(0, chunks)
    def _(q):
        gather(q, side, True)
        combine(side, True)
        gather(q, 1 - side, False)
        combine(1 - side, False)
        kept = (1 - flags[:, pl.ds(pl.multiple_of(q * LANES, LANES), LANES)]).astype(jnp.float32)
        count = jnp.maximum(jnp.sum(kept, axis=0, keepdims=True), 1.0)
        result = power[...].T / count
        for j in range(n):
            out_send[q, j, 0:b_loc, :] = result[j * b_loc:(j + 1) * b_loc].astype(jnp.bfloat16)

        @pl.loop(0, n - 1)
        def _(i):
            power_copy(q, partner(i), me).start()

    @pl.loop(0, chunks)
    def _(q):
        out[:, pl.ds(pl.multiple_of(me * width + q * LANES, LANES), LANES)] = out_send[q, me, 0:b_loc, :].astype(jnp.float32)

        @pl.loop(0, n - 1)
        def _(i):
            j = partner(i)
            power_copy(q, j, j).wait_recv()
            out[:, pl.ds(pl.multiple_of(j * width + q * LANES, LANES), LANES)] = out_recv[q, j, 0:b_loc, :].astype(jnp.float32)
            power_copy(q, j, me).wait_send()
            volt_copy(q, j, me).wait_send()


def local(n, voltages, jones_terms, rfi_flags, delay_ticks):
    _, s_loc, tsamp, channels = voltages.shape
    beams, stations = delay_ticks.shape
    chunks = channels // n // LANES
    b_loc = beams // n
    b_pad = -(-b_loc // 16) * 16
    rows = 4 * tsamp
    dims = (n, s_loc, tsamp, chunks, beams, stations, channels)
    f32, bf16 = jnp.float32, jnp.bfloat16
    anywhere = pl.BlockSpec(memory_space=pl.ANY)
    vmem = pl.BlockSpec(memory_space=pltpu.VMEM)
    dma = pltpu.SemaphoreType.DMA
    return pl.pallas_call(
        functools.partial(kernel, dims),
        out_shape=jax.ShapeDtypeStruct((b_loc, channels), f32),
        in_specs=[anywhere, anywhere, vmem, vmem],
        out_specs=vmem,
        scratch_shapes=[
            pltpu.VMEM((4 * s_loc * tsamp, channels), bf16),
            pltpu.VMEM((8 * s_loc, channels), bf16),
            pltpu.VMEM((8 * s_loc, LANES), f32),
            pltpu.VMEM((chunks, n, s_loc, rows, LANES), bf16),
            pltpu.VMEM((chunks, n, s_loc, rows, LANES), bf16),
            pltpu.VMEM((LANES * PITCH, LANES), f32),
            pltpu.VMEM((LANES * PITCH, LANES), f32),
            pltpu.VMEM((stations, beams), jnp.int32),
            pltpu.VMEM((LANES * rows, beams), f32),
            pltpu.VMEM((2, stations, beams), f32),
            pltpu.VMEM((PAIRS + 1, 2, stations, beams), f32),
            pltpu.VMEM((LANES, beams), f32),
            pltpu.VMEM((chunks, n, b_pad, LANES), bf16),
            pltpu.VMEM((chunks, n, b_pad, LANES), bf16),
            dma((n,)), dma((n,)),
            dma((chunks, n)), dma((chunks, n)), dma((chunks, n)), dma((chunks, n)),
        ],
        compiler_params=pltpu.CompilerParams(
            collective_id=0, has_side_effects=True, vmem_limit_bytes=56 * 1024 * 1024),
    )(
        voltages.reshape(4 * s_loc * tsamp, channels),
        jones_terms.reshape(8 * s_loc, channels),
        rfi_flags,
        delay_ticks,
    )


def solution(mesh):
    return jax.shard_map(
        functools.partial(local, mesh.shape["chan"]),
        mesh=mesh,
        in_specs=(
            P(None, "chan", "groups", None),
            P("groups", "chan", None),
            P("groups", "chan"),
            P(),
        ),
        out_specs=P("chan", "groups"),
        check_vma=False,
    )
```
